32 devices in a mesh: section: 4 (over y, x), dp: 8 (over z, core).
Axes of the slice: x: 2, y: 2, z: 4, core: 2. Of those that a mesh axis runs over, the one named last changes fastest.
Arguments:
- hidden: bfloat16 [8, 256, 8192], P('dp', 'section'), may hold values from -1500 to 1500
- head: bfloat16 [16384, 8192], P('section', 'dp'), may hold values from -0.0625 to 0.0625
- block_id: int32 [8, 4], P(None, 'section'), may hold values from 0 to 7
- block_live: int32 [8, 4], P(None, 'section'), may hold values from 0 to 1, as said below
- teacher: bfloat16 [8, 256, 2048], P('dp', None, 'section'), may hold values from -400 to 400
Outputs:
- grad_hidden: bfloat16 [8, 256, 8192], P('dp', 'section')
- grad_head: bfloat16 [16384, 8192], P('section', 'dp')
The draws below stay inside these ranges and needn't reach their ends.
Inputs may be any that keep to these rules, and one draw needn't show every extreme that they name: `block_live`: every micro-batch has at least one live section.
All inputs are finite; a program needn't handle non-finite values.
Results may differ from the reference program's by a relative error of at most 0.0056.
Values may be sent and summed in bfloat16 or wider, within the bound.
A program may use at most 128 MiB of HBM per device.

```python
import jax
import jax.numpy as jnp
from jax import lax

D = 8192
VB = 512
BLK_DEV = 8
TOK = 256
MBS = 8
V = 16384
N_SECTION = 4


def draw_hidden(key, part):
    base = jax.random.normal(jax.random.fold_in(key, 11), (MBS, TOK, D), jnp.float32)
    return base.astype(jnp.bfloat16)


def draw_teacher(key, part):
    base = 3.0 * jax.random.normal(jax.random.fold_in(key, 21), (MBS, TOK, N_SECTION * VB), jnp.float32)
    return base.astype(jnp.bfloat16)


def draw_block_live(key, part):
    rolls = jax.random.randint(jax.random.fold_in(key, 31), (MBS, N_SECTION), 0, 10)
    section_pos = jnp.arange(N_SECTION, dtype=jnp.int32)[None, :]
    batch_pos = jnp.arange(MBS, dtype=jnp.int32)[:, None]
    forced = section_pos == batch_pos % N_SECTION
    return ((rolls < 7) | forced).astype(jnp.int32)


def place_ends(entries, key, least, largest):
    longest = entries.shape.index(max(entries.shape))
    spots = []
    for shift in (0, 1):
        where = [jax.random.randint(jax.random.fold_in(key, axis), (), 0, length) for axis, length in enumerate(entries.shape)]
        where[longest] = (where[longest] + shift) % entries.shape[longest]
        spots.append(tuple(where))
    return entries.at[spots[0]].set(least).at[spots[1]].set(largest)


def level_of(rng, dims, split, smallest, largest):
    level, own = 1.0, jax.random.fold_in(rng, 6)
    for axis_at, blocks in split:
        draws = jnp.exp(jax.random.uniform(jax.random.fold_in(own, axis_at), (blocks,), jnp.float32, smallest / len(split), largest / len(split)))
        level = level * jnp.repeat(draws, dims[axis_at] // blocks).reshape([-1 if axis == axis_at else 1 for axis in range(len(dims))])
    return level


def bell_draw(stream_key, shape, deviation, most, pieces=(), kind=jnp.bfloat16):
    entries = jax.random.normal(stream_key, shape, jnp.float32) * deviation
    if len(pieces) > 0:
        entries = level_of(stream_key, shape, pieces, -0.22, 0.18) * entries
    return jnp.clip(entries, min=-most, max=most).astype(kind)


def setup_inputs(seed: int = 0) -> dict:
    seeds = jax.random.split(jax.random.key(seed), 6)
    return {
        "hidden": draw_hidden(jax.random.fold_in(seeds[5], 71), 0),
        "head": bell_draw(seeds[1], (V, D), D ** -0.5, 0.0625, ((0, 4), (1, 8))),
        "block_id": place_ends(jax.random.randint(seeds[2], (MBS, N_SECTION), 0, BLK_DEV), jax.random.fold_in(seeds[2], 1), 0, BLK_DEV - 1).astype(jnp.int32),
        "block_live": draw_block_live(jax.random.fold_in(seeds[5], 71), 0),
        "teacher": draw_teacher(jax.random.fold_in(seeds[5], 71), 0),
    }


neg_fill = -1.0e30


def reference(hidden, head, block_id, block_live, teacher):
    table = head.reshape(N_SECTION * BLK_DEV, VB, D)
    offsets = (jnp.arange(N_SECTION, dtype=jnp.int32) * BLK_DEV)[None, :]
    chosen = (block_id + offsets).astype(jnp.int32)
    counts = jnp.sum(block_live, axis=1).astype(jnp.float32)

    def forward(item):
        rows_hidden, picks, flags, scores, total = item
        rows = table[picks].astype(jnp.float32)
        logits = jnp.einsum("td,srd->tsr", rows_hidden.astype(jnp.float32), rows)
        mask = (flags > 0)[None, :, None]
        teach = scores.reshape(TOK, N_SECTION, VB).astype(jnp.float32)

        def probs(values):
            masked = jnp.where(mask, values, neg_fill)
            top = jnp.max(masked, axis=(1, 2), keepdims=True)
            expo = jnp.where(mask, jnp.exp(values - top), 0.0)
            return expo / jnp.sum(expo, axis=(1, 2), keepdims=True)

        grad = (VB * total * (probs(logits) - probs(teach))).astype(jnp.bfloat16)
        ghid = jnp.einsum("tsr,srd->td", grad.astype(jnp.float32), rows).astype(jnp.bfloat16)
        return grad, ghid

    logit_grad, grad_hidden = lax.map(forward, (hidden, chosen, block_live, teacher, counts))

    def per_section(section):
        grads = lax.dynamic_index_in_dim(logit_grad, section, 2, keepdims=False)
        contrib = jnp.einsum("mtr,mtd->mrd", grads.astype(jnp.float32), hidden.astype(jnp.float32)).astype(jnp.bfloat16)
        ids = lax.dynamic_index_in_dim(block_id, section, 1, keepdims=False)
        flags = lax.dynamic_index_in_dim(block_live, section, 1, keepdims=False)
        select = jnp.where((flags[:, None] > 0) & (ids[:, None] == jnp.arange(BLK_DEV, dtype=jnp.int32)[None, :]), 1.0, 0.0).astype(jnp.float32)
        return jnp.einsum("mb,mrd->brd", select, contrib.astype(jnp.float32)).astype(jnp.bfloat16)

    grad_head = lax.map(per_section, jnp.arange(N_SECTION, dtype=jnp.int32)).reshape(V, D)
    return grad_hidden, grad_head
```

```python
import functools

import jax
import jax.numpy as jnp
from jax import lax
from jax.experimental import pallas as pl
from jax.experimental.pallas import tpu as pltpu
from jax.sharding import PartitionSpec as P

neg_fill = -1e30


def pick_body(ids, head_ref, out_ref):
    out_ref[0] = head_ref[...]


def pick_rows(block_ids, head, block_rows):
    width = head.shape[1]
    batches = block_ids.shape[0]
    return pl.pallas_call(
        pick_body,
        grid_spec=pltpu.PrefetchScalarGridSpec(
            num_scalar_prefetch=1,
            grid=(batches,),
            in_specs=[pl.BlockSpec((block_rows, width), lambda m, ids: (ids[m], 0))],
            out_specs=pl.BlockSpec((1, block_rows, width), lambda m, ids: (m, 0, 0)),
        ),
        out_shape=jax.ShapeDtypeStruct((batches, block_rows, width), head.dtype),
        cost_estimate=pl.CostEstimate(
            flops=0, bytes_accessed=4 * batches * block_rows * width, transcendentals=0
        ),
    )(block_ids, head)


def head_body(ids, live, grad_ref, hid_ref, out_ref, acc):
    block = pl.program_id(0)
    batches = grad_ref.shape[0]
    acc[...] = jnp.zeros_like(acc)

    def step(m, carry):
        @pl.when(jnp.logical_and(live[m] > 0, ids[m] == block))
        def _():
            term = lax.dot_general(
                grad_ref[m], hid_ref[m], (((0,), (0,)), ((), ())),
                preferred_element_type=jnp.float32,
            )
            acc[...] += term.astype(jnp.bfloat16).astype(jnp.float32)

        return carry

    lax.fori_loop(0, batches, step, 0)
    out_ref[...] = acc[...].astype(out_ref.dtype)


def head_grad(block_ids, live_flags, grad_all, hid_all, blocks):
    batches, tokens, block_rows = grad_all.shape
    width = hid_all.shape[2]
    return pl.pallas_call(
        head_body,
        grid_spec=pltpu.PrefetchScalarGridSpec(
            num_scalar_prefetch=2,
            grid=(blocks,),
            in_specs=[
                pl.BlockSpec(grad_all.shape, lambda b, ids, live: (0, 0, 0)),
                pl.BlockSpec(hid_all.shape, lambda b, ids, live: (0, 0, 0)),
            ],
            out_specs=pl.BlockSpec((block_rows, width), lambda b, ids, live: (b, 0)),
            scratch_shapes=[pltpu.VMEM((block_rows, width), jnp.float32)],
        ),
        out_shape=jax.ShapeDtypeStruct((blocks * block_rows, width), jnp.bfloat16),
        compiler_params=pltpu.CompilerParams(vmem_limit_bytes=48 * 2**20),
        cost_estimate=pl.CostEstimate(
            flops=2 * batches * tokens * block_rows * width,
            bytes_accessed=2 * (grad_all.size + hid_all.size + blocks * block_rows * width),
            transcendentals=0,
        ),
    )(block_ids, live_flags, grad_all, hid_all)


def local(hidden, head, block_id, block_live, teacher):
    my_replica = lax.axis_index("dp")
    block_rows = teacher.shape[2]
    blocks = head.shape[0] // block_rows
    block_ids = block_id[:, 0]
    live_flags = block_live[:, 0]
    picked = pick_rows(block_ids, head, block_rows)
    mine = lax.all_to_all(hidden, "dp", split_axis=2, concat_axis=0, tiled=True)
    hid_all = lax.all_gather(mine, "section", axis=1, tiled=True)
    own_live = lax.dynamic_index_in_dim(live_flags, my_replica, 0, keepdims=False) > 0
    partial = jnp.einsum("mtd,mrd->mtr", hid_all, picked, preferred_element_type=jnp.float32)
    logits = lax.psum_scatter(partial, "dp", scatter_dimension=0, tiled=True)[0]
    teach = teacher[0].astype(jnp.float32)
    live_value = jnp.where(own_live, 1.0, 0.0).astype(jnp.float32)
    stud_local = jnp.where(own_live, jnp.max(logits, axis=1), neg_fill)
    teach_local = jnp.where(own_live, jnp.max(teach, axis=1), neg_fill)
    stud_top, teach_top = lax.pmax((stud_local, teach_local), "section")
    stud_part = jnp.where(own_live, jnp.sum(jnp.exp(logits - stud_top[:, None]), axis=1), 0.0)
    teach_part = jnp.where(own_live, jnp.sum(jnp.exp(teach - teach_top[:, None]), axis=1), 0.0)
    stud_total, teach_total, live_count = lax.psum((stud_part, teach_part, live_value), "section")
    student = jnp.where(own_live, jnp.exp(logits - stud_top[:, None]) / stud_total[:, None], 0.0)
    teach_prob = jnp.where(
        own_live, jnp.exp(teach - teach_top[:, None]) / teach_total[:, None], 0.0
    )
    logit_grad = (block_rows * live_count * (student - teach_prob)).astype(jnp.bfloat16)
    grad_all = lax.all_gather(logit_grad, "dp", axis=0)
    terms = jnp.einsum("mtr,mrd->mtd", grad_all, picked, preferred_element_type=jnp.float32)
    summed = lax.psum_scatter(terms, "section", scatter_dimension=1, tiled=True)
    grad_hidden = lax.all_to_all(
        summed.astype(jnp.bfloat16), "dp", split_axis=0, concat_axis=2, tiled=True
    )
    grad_head = head_grad(block_ids, live_flags, grad_all, hid_all, blocks)
    return (grad_hidden, grad_head)


def solution(mesh):
    placed = (
        P("dp", "section", None),
        P("section", "dp"),
        P(None, "section"),
        P(None, "section"),
        P("dp", None, "section"),
    )
    return jax.shard_map(
        local,
        mesh=mesh,
        in_specs=placed,
        out_specs=(P("dp", "section", None), P("section", "dp")),
        check_vma=False,
    )
```

```python
import functools

import jax
import jax.numpy as jnp
from jax import lax
from jax.experimental import pallas as pl
from jax.experimental.pallas import tpu as pltpu
from jax.sharding import PartitionSpec as P

neg_fill = -1e30


def pick_body(ids, head_ref, out_ref):
    out_ref[0] = head_ref[...]


def pick_rows(block_ids, head, block_rows):
    width = head.shape[1]
    batches = block_ids.shape[0]
    return pl.pallas_call(
        pick_body,
        grid_spec=pltpu.PrefetchScalarGridSpec(
            num_scalar_prefetch=1,
            grid=(batches,),
            in_specs=[pl.BlockSpec((block_rows, width), lambda m, ids: (ids[m], 0))],
            out_specs=pl.BlockSpec((1, block_rows, width), lambda m, ids: (m, 0, 0)),
        ),
        out_shape=jax.ShapeDtypeStruct((batches, block_rows, width), head.dtype),
        cost_estimate=pl.CostEstimate(
            flops=0, bytes_accessed=4 * batches * block_rows * width, transcendentals=0
        ),
    )(block_ids, head)


def head_body(ids, live, grad_ref, hid_ref, out_ref, acc):
    block = pl.program_id(0)
    batches = grad_ref.shape[0]
    acc[...] = jnp.zeros_like(acc)

    def step(m, carry):
        @pl.when(jnp.logical_and(live[m] > 0, ids[m] == block))
        def _():
            term = lax.dot_general(
                grad_ref[m], hid_ref[m], (((0,), (0,)), ((), ())),
                preferred_element_type=jnp.float32,
            )
            acc[...] += term.astype(jnp.bfloat16).astype(jnp.float32)

        return carry

    lax.fori_loop(0, batches, step, 0)
    out_ref[...] = acc[...].astype(out_ref.dtype)


def head_grad(block_ids, live_flags, grad_all, hid_all, blocks):
    batches, tokens, block_rows = grad_all.shape
    width = hid_all.shape[2]
    return pl.pallas_call(
        head_body,
        grid_spec=pltpu.PrefetchScalarGridSpec(
            num_scalar_prefetch=2,
            grid=(blocks,),
            in_specs=[
                pl.BlockSpec(grad_all.shape, lambda b, ids, live: (0, 0, 0)),
                pl.BlockSpec(hid_all.shape, lambda b, ids, live: (0, 0, 0)),
            ],
            out_specs=pl.BlockSpec((block_rows, width), lambda b, ids, live: (b, 0)),
            scratch_shapes=[pltpu.VMEM((block_rows, width), jnp.float32)],
        ),
        out_shape=jax.ShapeDtypeStruct((blocks * block_rows, width), jnp.bfloat16),
        compiler_params=pltpu.CompilerParams(vmem_limit_bytes=48 * 2**20),
        cost_estimate=pl.CostEstimate(
            flops=2 * batches * tokens * block_rows * width,
            bytes_accessed=2 * (grad_all.size + hid_all.size + blocks * block_rows * width),
            transcendentals=0,
        ),
    )(block_ids, live_flags, grad_all, hid_all)


MESH = pl.DeviceIdType.MESH


def exchange_body(
    hidden, picked, teacher, live, hid_all, grad_all, hid_grad,
    pair_out, pair_in, chip_sum, chip_in, stat_out, stat_in, coef,
    term_out, term_in, term_own, final,
    a1s, a1r, a2s, a2r, cs, cr, zs, zr, ss, sr, gs, gr, fs, e1s, e1r, e2s, e2r,
):
    sec = lax.axis_index("section")
    rep = lax.axis_index("dp")
    batches, tokens, width = hid_all.shape
    n_sec = stat_in.shape[0]
    chips = batches // 2
    tok_local = tokens // n_sec
    block_rows = picked.shape[1]
    core = lax.rem(rep, 2)
    z = rep // 2
    sib = 2 * z + 1 - core
    f32, bf16 = jnp.float32, jnp.bfloat16

    def chip_at(k):
        return lax.rem(z + k, chips)

    def chip_back(k):
        return lax.rem(z - k + chips, chips)

    def sec_at(j):
        return lax.rem(sec + j, n_sec)

    def rows_of(s):
        return pl.ds(pl.multiple_of(s * tok_local, tok_local), tok_local)

    def cols_of(d):
        return pl.ds(pl.multiple_of(d * width, width), width)

    def loop(lo, hi, body):
        def step(i, carry):
            body(i)
            return carry

        lax.fori_loop(lo, hi, step, 0)

    def remote(src, dst, send, recv, **to):
        return pltpu.make_async_remote_copy(
            src_ref=src, dst_ref=dst, send_sem=send, recv_sem=recv,
            device_id=to, device_id_type=MESH,
        )

    barrier = pltpu.get_barrier_semaphore()

    def hello_dp(k):
        pl.semaphore_signal(barrier, inc=1, device_id={"dp": lax.rem(rep + k, batches)}, device_id_type=MESH)

    def hello_sec(j):
        pl.semaphore_signal(barrier, inc=1, device_id={"section": sec_at(j)}, device_id_type=MESH)

    loop(1, batches, hello_dp)
    loop(1, n_sec, hello_sec)
    pl.semaphore_wait(barrier, batches - 1 + n_sec - 1)

    def piece(to, source):
        return remote(
            hidden.at[0, :, cols_of(to)], hid_all.at[source, rows_of(sec), :],
            a1s.at[to], a1r.at[source], dp=to,
        )

    piece(sib, rep).start()

    def send_piece(k):
        piece(2 * chip_back(k) + core, rep).start()
        piece(2 * chip_back(k) + 1 - core, rep).start()

    loop(1, chips, send_piece)
    hid_all[rep, rows_of(sec), :] = hidden[0, :, cols_of(rep)]

    def spread(m, s_to, s_from):
        block = hid_all.at[m, rows_of(s_from), :]
        return remote(block, block, a2s.at[m, s_to], a2r.at[m, s_from], section=s_to)

    def forward(m):
        loop(1, n_sec, lambda j: spread(m, sec_at(j), sec).start())

    def arrive(m):
        loop(1, n_sec, lambda j: spread(m, sec_at(j), sec_at(j)).wait_recv())

    def forward_chip(k):
        for parity in (core, 1 - core):
            m = 2 * chip_at(k) + parity
            piece(sib, m).wait_recv()
            forward(m)

    forward(rep)
    piece(sib, sib).wait_recv()
    forward(sib)
    forward_chip(1)

    def scores(m):
        return lax.dot_general(
            hid_all[m], picked[m], (((1,), (1,)), ((), ())), preferred_element_type=f32
        )

    def pair(zz):
        return remote(pair_out.at[zz], pair_in.at[zz], cs.at[zz], cr.at[zz], dp=sib)

    def owner(zz, source):
        return remote(
            chip_sum.at[zz], chip_in.at[source], zs.at[zz], zr.at[source], dp=2 * zz + core
        )

    def logits_of(k):
        @pl.when(k < chips - 2)
        def _():
            forward_chip(k + 2)

        zz = chip_at(k)
        away, near = 2 * zz + 1 - core, 2 * zz + core
        arrive(away)
        pair_out[zz] = scores(away)
        pair(zz).start()
        arrive(near)
        value = scores(near)
        pair(zz).wait_recv()
        chip_sum[zz] = value + pair_in[zz]

        @pl.when(k > 0)
        def _():
            owner(zz, z).start()

    loop(0, chips, logits_of)

    def collect(k):
        owner(chip_at(k), chip_at(k)).wait_recv()
        chip_sum[z] = chip_sum[z] + chip_in[chip_at(k)]

    loop(1, chips, collect)

    logits = chip_sum[z]
    teach = teacher[0].astype(f32)
    s_max = jnp.max(logits, axis=1, keepdims=True)
    t_max = jnp.max(teach, axis=1, keepdims=True)
    s_exp = jnp.exp(logits - s_max)
    t_exp = jnp.exp(teach - t_max)
    s_sum = jnp.sum(s_exp, axis=1, keepdims=True)
    t_sum = jnp.sum(t_exp, axis=1, keepdims=True)
    lane = lax.broadcasted_iota(jnp.int32, (tokens, 128), 1)
    stats = jnp.where(lane == 0, s_max, 0.0)
    stats = jnp.where(lane == 1, s_sum, stats)
    stats = jnp.where(lane == 2, t_max, stats)
    stats = jnp.where(lane == 3, t_sum, stats)
    rows = stats.T[:8]
    row_at = lax.broadcasted_iota(jnp.int32, rows.shape, 0)
    rows = jnp.where(row_at == 4, live[...], rows)
    stat_out[...] = rows
    stat_in[sec] = rows

    def stat(s_to, s_from):
        return remote(stat_out, stat_in.at[s_from], ss.at[s_to], sr.at[s_from], section=s_to)

    loop(1, n_sec, lambda j: stat(sec_at(j), sec).start())
    loop(1, n_sec, lambda j: stat(sec_at(j), sec_at(j)).wait_recv())
    alive = [stat_in[i, 4:5, :] for i in range(n_sec)]
    count = functools.reduce(jnp.add, alive)

    def merged(at):
        tops = [jnp.where(a > 0, stat_in[i, at : at + 1, :], neg_fill) for i, a in enumerate(alive)]
        top = functools.reduce(jnp.maximum, tops)
        total = functools.reduce(
            jnp.add,
            [
                jnp.where(a > 0, stat_in[i, at + 1 : at + 2, :] * jnp.exp(tops[i] - top), 0.0)
                for i, a in enumerate(alive)
            ],
        )
        own = stat_in[sec]
        own_alive = own[4:5, :] > 0
        own_top = jnp.where(own_alive, own[at : at + 1, :], neg_fill)
        return jnp.where(own_alive, block_rows * count * (jnp.exp(own_top - top) / total), 0.0)

    coef[...] = jnp.zeros_like(coef)
    coef[0:1, :] = merged(0)
    coef[1:2, :] = merged(2)
    turned = coef[...].T
    grad_all[rep] = (s_exp * turned[:, 0:1] - t_exp * turned[:, 1:2]).astype(bf16)

    def share(zz, m):
        return remote(grad_all.at[m], grad_all.at[m], gs.at[zz], gr.at[m], dp=2 * zz + core)

    def relay(m):
        return remote(grad_all.at[m], grad_all.at[m], fs.at[m // 2], gr.at[m], dp=sib)

    relay(rep).start()
    loop(1, chips, lambda k: share(chip_back(k), rep).start())

    def term(m, s_to, s_from):
        return remote(
            term_out.at[m, rows_of(s_to), :], term_in.at[m, s_from],
            e1s.at[m, s_to], e1r.at[m, s_from], section=s_to,
        )

    def terms_of(m):
        value = lax.dot_general(
            grad_all[m], picked[m], (((1,), (0,)), ((), ())), preferred_element_type=f32
        )
        term_out[m] = value.astype(bf16)
        loop(1, n_sec, lambda j: term(m, sec_at(j), sec).start())
        term_own[m] = lax.dot_general(
            grad_all[m, rows_of(sec), :], picked[m], (((1,), (0,)), ((), ())),
            preferred_element_type=f32,
        )

    def terms_chip(k):
        near, away = 2 * chip_at(k) + core, 2 * chip_at(k) + 1 - core

        @pl.when(k > 0)
        def _():
            share(chip_at(k), near).wait_recv()
            relay(near).start()

        terms_of(near)
        relay(away).wait_recv()
        terms_of(away)

    loop(0, chips, terms_chip)

    def home(m, source):
        return remote(
            final.at[m], hid_grad.at[:, cols_of(source)], e2s.at[m], e2r.at[source], dp=m
        )

    def summed(m):
        loop(1, n_sec, lambda j: term(m, sec_at(j), sec_at(j)).wait_recv())

        def add(j):
            term_own[m] = term_own[m] + term_in[m, sec_at(j)].astype(f32)

        loop(1, n_sec, add)
        return term_own[m].astype(bf16)

    hid_grad[:, cols_of(rep)] = summed(rep)
    final[sib] = summed(sib)
    home(sib, rep).start()

    def finish(k):
        for parity in (core, 1 - core):
            m = 2 * chip_at(k) + parity
            final[m] = summed(m)
            home(m, rep).start()

    loop(1, chips, finish)

    def ends_dp(k):
        other = lax.rem(rep + k, batches)
        home(other, other).wait_recv()
        home(other, rep).wait_send()
        piece(other, rep).wait_send()

    loop(1, batches, ends_dp)

    def ends_all(m):
        def each(j):
            spread(m, sec_at(j), sec).wait_send()
            term(m, sec_at(j), sec).wait_send()

        loop(1, n_sec, each)

    loop(0, batches, ends_all)
    loop(1, n_sec, lambda j: stat(sec_at(j), sec).wait_send())

    def ends_chip(k):
        pair(chip_at(k)).wait_send()
        relay(2 * chip_at(k) + core).wait_send()

        @pl.when(k > 0)
        def _():
            owner(chip_at(k), z).wait_send()
            share(chip_at(k), rep).wait_send()

    loop(0, chips, ends_chip)


def exchange(hidden, picked, teacher, live, n_sec):
    tok_local, model_width = hidden.shape[1], hidden.shape[2]
    batches, block_rows, width = picked.shape
    tokens = teacher.shape[1]
    chips = batches // 2
    dma = pltpu.SemaphoreType.DMA
    f32, bf16 = jnp.float32, jnp.bfloat16
    vmem = pl.BlockSpec(memory_space=pltpu.VMEM)
    return pl.pallas_call(
        exchange_body,
        out_shape=(
            jax.ShapeDtypeStruct((batches, tokens, width), bf16),
            jax.ShapeDtypeStruct((batches, tokens, block_rows), bf16),
            jax.ShapeDtypeStruct((tok_local, model_width), bf16),
        ),
        in_specs=[vmem] * 4,
        out_specs=(vmem,) * 3,
        scratch_shapes=[
            pltpu.VMEM((chips, tokens, block_rows), f32),
            pltpu.VMEM((chips, tokens, block_rows), f32),
            pltpu.VMEM((chips, tokens, block_rows), f32),
            pltpu.VMEM((chips, tokens, block_rows), f32),
            pltpu.VMEM((8, tokens), f32),
            pltpu.VMEM((n_sec, 8, tokens), f32),
            pltpu.VMEM((128, tokens), f32),
            pltpu.VMEM((batches, tokens, width), bf16),
            pltpu.VMEM((batches, n_sec, tok_local, width), bf16),
            pltpu.VMEM((batches, tok_local, width), f32),
            pltpu.VMEM((batches, tok_local, width), bf16),
            dma((batches,)), dma((batches,)),
            dma((batches, n_sec)), dma((batches, n_sec)),
            dma((chips,)), dma((chips,)),
            dma((chips,)), dma((chips,)),
            dma((n_sec,)), dma((n_sec,)),
            dma((chips,)), dma((batches,)), dma((chips,)),
            dma((batches, n_sec)), dma((batches, n_sec)),
            dma((batches,)), dma((batches,)),
        ],
        compiler_params=pltpu.CompilerParams(
            collective_id=0, has_side_effects=True, vmem_limit_bytes=60 * 2**20
        ),
        cost_estimate=pl.CostEstimate(
            flops=4 * batches * tokens * block_rows * width,
            bytes_accessed=2 * batches * block_rows * width,
            transcendentals=0,
        ),
    )(hidden, picked, teacher, live)


def local(hidden, head, block_id, block_live, teacher, n_sec):
    my_replica = lax.axis_index("dp")
    tokens, block_rows = teacher.shape[1], teacher.shape[2]
    blocks = head.shape[0] // block_rows
    block_ids = block_id[:, 0]
    live_flags = block_live[:, 0]
    picked = pick_rows(block_ids, head, block_rows)
    own_live = lax.dynamic_index_in_dim(live_flags, my_replica, 0, keepdims=False) > 0
    live = jnp.broadcast_to(jnp.where(own_live, 1.0, 0.0).astype(jnp.float32), (8, tokens))
    hid_all, grad_all, hid_grad = exchange(hidden, picked, teacher, live, n_sec)
    grad_head = head_grad(block_ids, live_flags, grad_all, hid_all, blocks)
    return (hid_grad[None], grad_head)


def solution(mesh):
    placed = (
        P("dp", "section", None),
        P("section", "dp"),
        P(None, "section"),
        P(None, "section"),
        P("dp", None, "section"),
    )
    return jax.shard_map(
        functools.partial(local, n_sec=mesh.shape["section"]),
        mesh=mesh,
        in_specs=placed,
        out_specs=(P("dp", "section", None), P("section", "dp")),
        check_vma=False,
    )
```

```python
import functools

import jax
import jax.numpy as jnp
from jax import lax
from jax.experimental import pallas as pl
from jax.experimental.pallas import tpu as pltpu
from jax.sharding import PartitionSpec as P

neg_fill = -1e30


def head_body(ids, live, grad_ref, hid_ref, out_ref, acc):
    block = pl.program_id(0)
    batches = grad_ref.shape[0]

    def step(m, hits):
        match = jnp.logical_and(live[m] > 0, ids[m] == block)

        def term():
            return lax.dot_general(
                grad_ref[m], hid_ref[m], (((0,), (0,)), ((), ())),
                preferred_element_type=jnp.float32,
            ).astype(jnp.bfloat16)

        @pl.when(jnp.logical_and(match, hits == 0))
        def _():
            out_ref[...] = term()

        @pl.when(jnp.logical_and(match, hits > 0))
        def _():
            @pl.when(hits == 1)
            def _():
                acc[...] = out_ref[...].astype(jnp.float32)

            acc[...] += term().astype(jnp.float32)

        return hits + match.astype(jnp.int32)

    hits = lax.fori_loop(0, batches, step, jnp.int32(0))

    @pl.when(hits == 0)
    def _():
        out_ref[...] = jnp.zeros_like(out_ref)

    @pl.when(hits > 1)
    def _():
        out_ref[...] = acc[...].astype(out_ref.dtype)


def head_grad(block_ids, live_flags, grad_all, hid_all, blocks):
    batches, tokens, block_rows = grad_all.shape
    width = hid_all.shape[2]
    return pl.pallas_call(
        head_body,
        grid_spec=pltpu.PrefetchScalarGridSpec(
            num_scalar_prefetch=2,
            grid=(blocks,),
            in_specs=[
                pl.BlockSpec(grad_all.shape, lambda b, ids, live: (0, 0, 0)),
                pl.BlockSpec(hid_all.shape, lambda b, ids, live: (0, 0, 0)),
            ],
            out_specs=pl.BlockSpec((block_rows, width), lambda b, ids, live: (b, 0)),
            scratch_shapes=[pltpu.VMEM((block_rows, width), jnp.float32)],
        ),
        out_shape=jax.ShapeDtypeStruct((blocks * block_rows, width), jnp.bfloat16),
        compiler_params=pltpu.CompilerParams(vmem_limit_bytes=48 * 2**20),
        cost_estimate=pl.CostEstimate(
            flops=2 * batches * tokens * block_rows * width,
            bytes_accessed=2 * (grad_all.size + hid_all.size + blocks * block_rows * width),
            transcendentals=0,
        ),
    )(block_ids, live_flags, grad_all, hid_all)


MESH = pl.DeviceIdType.MESH


def exchange_body(
    hidden, head, ids, teacher, live, hid_out, grad_out, hid_grad,
    table, hid_all, grad_all, value_all, term_mid,
    pair_out, pair_in, chip_sum, chip_in, stat_out, stat_in, coef,
    term_out, term_in, term_own, final,
    a1s, a1r, a2s, a2r, cs, cr, zs, zr, ss, sr, gs, gr, fs, e1s, e1r, e2s, e2r, own_sems,
):
    sec = lax.axis_index("section")
    rep = lax.axis_index("dp")
    batches, tokens, width = hid_all.shape
    n_sec = stat_in.shape[0]
    chips = batches // 2
    tok_local = tokens // n_sec
    block_rows = table.shape[1]
    core = lax.rem(rep, 2)
    z = rep // 2
    sib = 2 * z + 1 - core
    f32, bf16 = jnp.float32, jnp.bfloat16

    def chip_at(k):
        return lax.rem(z + k, chips)

    def chip_back(k):
        return lax.rem(z - k + chips, chips)

    def sec_at(j):
        return lax.rem(sec + j, n_sec)

    def rows_of(s):
        return pl.ds(pl.multiple_of(s * tok_local, tok_local), tok_local)

    def cols_of(d):
        return pl.ds(pl.multiple_of(d * width, width), width)

    def loop(lo, hi, body):
        def step(i, carry):
            body(i)
            return carry

        lax.fori_loop(lo, hi, step, 0)

    def remote(src, dst, send, recv, **to):
        return pltpu.make_async_remote_copy(
            src_ref=src, dst_ref=dst, send_sem=send, recv_sem=recv,
            device_id=to, device_id_type=MESH,
        )

    two_level = n_sec == 4
    x_next, y_next, across = sec + 1 - 2 * lax.rem(sec, 2), lax.rem(sec + 2, 4), 3 - sec

    def first_of(m):
        return x_next + lax.rem(m, 2) * (y_next - x_next)

    def second_of(m):
        return y_next + lax.rem(m, 2) * (x_next - y_next)

    load_head = pltpu.make_async_copy(head, table, own_sems.at[0])
    load_head.start()
    barrier = pltpu.get_barrier_semaphore()

    def hello_dp(k):
        pl.semaphore_signal(barrier, inc=1, device_id={"dp": lax.rem(rep + k, batches)}, device_id_type=MESH)

    def hello_sec(j):
        pl.semaphore_signal(barrier, inc=1, device_id={"section": sec_at(j)}, device_id_type=MESH)

    loop(1, batches, hello_dp)
    loop(1, n_sec, hello_sec)
    pl.semaphore_wait(barrier, batches - 1 + n_sec - 1)

    def piece(to, source):
        return remote(
            hidden.at[0, :, cols_of(to)], hid_all.at[source, rows_of(sec), :],
            a1s.at[to], a1r.at[source], dp=to,
        )

    piece(sib, rep).start()

    def send_piece(k):
        piece(2 * chip_back(k) + core, rep).start()
        piece(2 * chip_back(k) + 1 - core, rep).start()

    loop(1, chips, send_piece)
    hid_all[rep, rows_of(sec), :] = hidden[0, :, cols_of(rep)]

    def spread(m, s_to, s_from, slot):
        block = hid_all.at[m, rows_of(s_from), :]
        return remote(block, block, a2s.at[m, slot], a2r.at[m, s_from], section=s_to)

    def forward(m):
        if two_level:
            spread(m, first_of(m), sec, first_of(m)).start()
            spread(m, second_of(m), sec, second_of(m)).start()
        else:
            loop(1, n_sec, lambda j: spread(m, sec_at(j), sec, sec_at(j)).start())

    def pass_on(m):
        if two_level:
            spread(m, first_of(m), first_of(m), across).wait_recv()
            spread(m, second_of(m), first_of(m), across).start()

    def pass_chip(k):
        pass_on(2 * chip_at(k) + core)
        pass_on(2 * chip_at(k) + 1 - core)

    def arrive(m):
        if two_level:
            spread(m, second_of(m), second_of(m), across).wait_recv()
            spread(m, second_of(m), across, across).wait_recv()
        else:
            loop(1, n_sec, lambda j: spread(m, sec_at(j), sec_at(j), sec_at(j)).wait_recv())

    def forward_chip(k):
        for parity in (core, 1 - core):
            m = 2 * chip_at(k) + parity
            piece(sib, m).wait_recv()
            forward(m)

    forward(rep)
    piece(sib, sib).wait_recv()
    forward(sib)
    forward_chip(1)
    pass_chip(0)
    load_head.wait()

    def scores(m):
        return lax.dot_general(
            hid_all[m], table[ids[m]], (((1,), (1,)), ((), ())), preferred_element_type=f32
        )

    def pair(zz):
        return remote(pair_out.at[zz], pair_in.at[zz], cs.at[zz], cr.at[zz], dp=sib)

    def owner(zz, source):
        return remote(
            chip_sum.at[zz], chip_in.at[source], zs.at[zz], zr.at[source], dp=2 * zz + core
        )

    def logits_of(k):
        @pl.when(k < chips - 2)
        def _():
            forward_chip(k + 2)

        @pl.when(k < chips - 1)
        def _():
            pass_chip(k + 1)

        zz = chip_at(k)
        away, near = 2 * zz + 1 - core, 2 * zz + core
        arrive(away)
        pair_out[zz] = scores(away)
        pair(zz).start()
        arrive(near)
        value = scores(near)
        pair(zz).wait_recv()
        chip_sum[zz] = value + pair_in[zz]

        @pl.when(k > 0)
        def _():
            owner(zz, z).start()

    loop(0, chips, logits_of)
    save_hid = pltpu.make_async_copy(hid_all, hid_out, own_sems.at[1])
    save_hid.start()

    def collect(k):
        owner(chip_at(k), chip_at(k)).wait_recv()
        chip_sum[z] = chip_sum[z] + chip_in[chip_at(k)]

    loop(1, chips, collect)

    logits = chip_sum[z]
    teach = teacher[0].astype(f32)
    s_max = jnp.max(logits, axis=1, keepdims=True)
    t_max = jnp.max(teach, axis=1, keepdims=True)
    s_exp = jnp.exp(logits - s_max)
    t_exp = jnp.exp(teach - t_max)
    s_sum = jnp.sum(s_exp, axis=1, keepdims=True)
    t_sum = jnp.sum(t_exp, axis=1, keepdims=True)
    lane = lax.broadcasted_iota(jnp.int32, (tokens, 128), 1)
    stats = jnp.where(lane == 0, s_max, 0.0)
    stats = jnp.where(lane == 1, s_sum, stats)
    stats = jnp.where(lane == 2, t_max, stats)
    stats = jnp.where(lane == 3, t_sum, stats)
    rows = stats.T[:8]
    row_at = lax.broadcasted_iota(jnp.int32, rows.shape, 0)
    rows = jnp.where(row_at == 4, live[...], rows)
    stat_out[...] = rows
    stat_in[sec] = rows

    def stat(s_to, s_from):
        return remote(stat_out, stat_in.at[s_from], ss.at[s_to], sr.at[s_from], section=s_to)

    loop(1, n_sec, lambda j: stat(sec_at(j), sec).start())
    loop(1, n_sec, lambda j: stat(sec_at(j), sec_at(j)).wait_recv())
    alive = [stat_in[i, 4:5, :] for i in range(n_sec)]
    count = functools.reduce(jnp.add, alive)

    def merged(at):
        tops = [jnp.where(a > 0, stat_in[i, at : at + 1, :], neg_fill) for i, a in enumerate(alive)]
        top = functools.reduce(jnp.maximum, tops)
        total = functools.reduce(
            jnp.add,
            [
                jnp.where(a > 0, stat_in[i, at + 1 : at + 2, :] * jnp.exp(tops[i] - top), 0.0)
                for i, a in enumerate(alive)
            ],
        )
        own = stat_in[sec]
        own_alive = own[4:5, :] > 0
        own_top = jnp.where(own_alive, own[at : at + 1, :], neg_fill)
        return jnp.where(own_alive, block_rows * count * (jnp.exp(own_top - top) / total), 0.0)

    coef[...] = jnp.zeros_like(coef)
    coef[0:1, :] = merged(0)
    coef[1:2, :] = merged(2)
    turned = coef[...].T
    grad_all[rep] = (s_exp * turned[:, 0:1] - t_exp * turned[:, 1:2]).astype(bf16)

    def share(zz, m):
        return remote(grad_all.at[m], grad_all.at[m], gs.at[zz], gr.at[m], dp=2 * zz + core)

    def relay(m):
        return remote(grad_all.at[m], grad_all.at[m], fs.at[m // 2], gr.at[m], dp=sib)

    relay(rep).start()
    loop(1, chips, lambda k: share(chip_back(k), rep).start())

    def term(m, s_to, s_from):
        return remote(
            term_out.at[m, rows_of(s_to), :], term_in.at[m, s_from],
            e1s.at[m, s_to], e1r.at[m, s_from], section=s_to,
        )

    def passed(m, s_to, slot):
        return remote(
            term_out.at[m, rows_of(across), :], term_in.at[m, slot],
            e1s.at[m, across], e1r.at[m, slot], section=s_to,
        )

    def onward(m, s_to, s_from):
        return remote(
            term_out.at[m, rows_of(sec), :], term_in.at[m, s_from],
            e1s.at[m, s_to], e1r.at[m, s_from], section=s_to,
        )

    def terms_of(m):
        value = lax.dot_general(
            grad_all[m], table[ids[m]], (((1,), (0,)), ((), ())), preferred_element_type=f32
        )
        value_all[...] = value
        term_out[m] = value.astype(bf16)
        if two_level:
            passed(m, first_of(m), 3 - first_of(m)).start()
            term(m, first_of(m), sec).start()
            term_mid[m] = value_all[rows_of(second_of(m)), :]
        else:
            loop(1, n_sec, lambda j: term(m, sec_at(j), sec).start())
        term_own[m] = value_all[rows_of(sec), :]

    def terms_chip(k):
        near, away = 2 * chip_at(k) + core, 2 * chip_at(k) + 1 - core

        @pl.when(k > 0)
        def _():
            share(chip_at(k), near).wait_recv()
            relay(near).start()

        terms_of(near)
        relay(away).wait_recv()
        terms_of(away)

    def middle_of(m):
        passed(m, first_of(m), across).wait_recv()
        both = term_mid[m] + term_in[m, across].astype(f32)
        term_out[m, rows_of(sec), :] = both.astype(bf16)
        onward(m, second_of(m), sec).start()

    def middle_chip(k):
        if two_level:
            middle_of(2 * chip_at(k) + core)
            middle_of(2 * chip_at(k) + 1 - core)

    def home(m, source):
        return remote(
            final.at[m], hid_grad.at[:, cols_of(source)], e2s.at[m], e2r.at[source], dp=m
        )

    def summed(m):
        if two_level:
            term(m, first_of(m), first_of(m)).wait_recv()
            onward(m, second_of(m), second_of(m)).wait_recv()
            return (
                term_own[m]
                + term_in[m, first_of(m)].astype(f32)
                + term_in[m, second_of(m)].astype(f32)
            ).astype(bf16)
        loop(1, n_sec, lambda j: term(m, sec_at(j), sec_at(j)).wait_recv())

        def add(j):
            term_own[m] = term_own[m] + term_in[m, sec_at(j)].astype(f32)

        loop(1, n_sec, add)
        return term_own[m].astype(bf16)

    def finish(k):
        near, away = 2 * chip_at(k) + core, 2 * chip_at(k) + 1 - core
        final[near] = summed(near)

        @pl.when(k > 0)
        def _():
            home(near, rep).start()

        final[away] = summed(away)
        home(away, rep).start()

    def stage(i):
        @pl.when(i < chips)
        def _():
            terms_chip(i)

        @pl.when(jnp.logical_and(i > 0, i <= chips))
        def _():
            middle_chip(i - 1)

        @pl.when(i > 1)
        def _():
            finish(i - 2)

    loop(0, chips, stage)
    save_grad = pltpu.make_async_copy(grad_all, grad_out, own_sems.at[2])
    save_grad.start()
    loop(chips, chips + 2, stage)
    hid_grad[:, cols_of(rep)] = final[rep]

    def ends_dp(k):
        other = lax.rem(rep + k, batches)
        home(other, other).wait_recv()
        home(other, rep).wait_send()
        piece(other, rep).wait_send()

    loop(1, batches, ends_dp)

    def ends_all(m):
        def each(j):
            spread(m, sec_at(j), sec, sec_at(j)).wait_send()
            term(m, sec_at(j), sec).wait_send()

        loop(1, n_sec, each)

    loop(0, batches, ends_all)
    loop(1, n_sec, lambda j: stat(sec_at(j), sec).wait_send())

    def ends_chip(k):
        pair(chip_at(k)).wait_send()
        relay(2 * chip_at(k) + core).wait_send()

        @pl.when(k > 0)
        def _():
            owner(chip_at(k), z).wait_send()
            share(chip_at(k), rep).wait_send()

    loop(0, chips, ends_chip)
    save_hid.wait()
    save_grad.wait()


def exchange(hidden, table, ids, teacher, live, n_sec):
    tok_local, model_width = hidden.shape[1], hidden.shape[2]
    blocks, block_rows, width = table.shape
    batches = ids.shape[0]
    tokens = teacher.shape[1]
    chips = batches // 2
    dma = pltpu.SemaphoreType.DMA
    f32, bf16 = jnp.float32, jnp.bfloat16
    vmem = pl.BlockSpec(memory_space=pltpu.VMEM)
    smem = pl.BlockSpec(memory_space=pltpu.SMEM)
    hbm = pl.BlockSpec(memory_space=pl.ANY)
    return pl.pallas_call(
        exchange_body,
        out_shape=(
            jax.ShapeDtypeStruct((batches, tokens, width), bf16),
            jax.ShapeDtypeStruct((batches, tokens, block_rows), bf16),
            jax.ShapeDtypeStruct((tok_local, model_width), bf16),
        ),
        in_specs=[vmem, hbm, smem, vmem, vmem],
        out_specs=(hbm, hbm, vmem),
        scratch_shapes=[
            pltpu.VMEM((blocks, block_rows, width), bf16),
            pltpu.VMEM((batches, tokens, width), bf16),
            pltpu.VMEM((batches, tokens, block_rows), bf16),
            pltpu.VMEM((tokens, width), f32),
            pltpu.VMEM((batches, tok_local, width), f32),
            pltpu.VMEM((chips, tokens, block_rows), f32),
            pltpu.VMEM((chips, tokens, block_rows), f32),
            pltpu.VMEM((chips, tokens, block_rows), f32),
            pltpu.VMEM((chips, tokens, block_rows), f32),
            pltpu.VMEM((8, tokens), f32),
            pltpu.VMEM((n_sec, 8, tokens), f32),
            pltpu.VMEM((128, tokens), f32),
            pltpu.VMEM((batches, tokens, width), bf16),
            pltpu.VMEM((batches, n_sec, tok_local, width), bf16),
            pltpu.VMEM((batches, tok_local, width), f32),
            pltpu.VMEM((batches, tok_local, width), bf16),
            dma((batches,)), dma((batches,)),
            dma((batches, n_sec)), dma((batches, n_sec)),
            dma((chips,)), dma((chips,)),
            dma((chips,)), dma((chips,)),
            dma((n_sec,)), dma((n_sec,)),
            dma((chips,)), dma((batches,)), dma((chips,)),
            dma((batches, n_sec)), dma((batches, n_sec)),
            dma((batches,)), dma((batches,)), dma((3,)),
        ],
        compiler_params=pltpu.CompilerParams(
            collective_id=0, has_side_effects=True, vmem_limit_bytes=60 * 2**20
        ),
        cost_estimate=pl.CostEstimate(
            flops=4 * batches * tokens * block_rows * width,
            bytes_accessed=2 * batches * block_rows * width,
            transcendentals=0,
        ),
    )(hidden, table, ids, teacher, live)


def local(hidden, head, block_id, block_live, teacher, n_sec):
    my_replica = lax.axis_index("dp")
    tokens, block_rows = teacher.shape[1], teacher.shape[2]
    blocks = head.shape[0] // block_rows
    block_ids = block_id[:, 0]
    live_flags = block_live[:, 0]
    table = head.reshape(blocks, block_rows, head.shape[1])
    own_live = lax.dynamic_index_in_dim(live_flags, my_replica, 0, keepdims=False) > 0
    live = jnp.broadcast_to(jnp.where(own_live, 1.0, 0.0).astype(jnp.float32), (8, tokens))
    hid_all, grad_all, hid_grad = exchange(hidden, table, block_ids, teacher, live, n_sec)
    grad_head = head_grad(block_ids, live_flags, grad_all, hid_all, blocks)
    return (hid_grad[None], grad_head)


def solution(mesh):
    placed = (
        P("dp", "section", None),
        P("section", "dp"),
        P(None, "section"),
        P(None, "section"),
        P("dp", None, "section"),
    )
    return jax.shard_map(
        functools.partial(local, n_sec=mesh.shape["section"]),
        mesh=mesh,
        in_specs=placed,
        out_specs=(P("dp", "section", None), P("section", "dp")),
        check_vma=False,
    )
```

```python
import functools

import jax
import jax.numpy as jnp
from jax import lax
from jax.experimental import pallas as pl
from jax.experimental.pallas import tpu as pltpu
from jax.sharding import PartitionSpec as P

neg_fill = -1e30


def head_body(ids, live, grad_ref, hid_ref, out_ref, acc):
    block = pl.program_id(0)
    batches = grad_ref.shape[0]

    def step(m, hits):
        match = jnp.logical_and(live[m] > 0, ids[m] == block)

        def term():
            return lax.dot_general(
                grad_ref[m], hid_ref[m], (((0,), (0,)), ((), ())),
                preferred_element_type=jnp.float32,
            ).astype(jnp.bfloat16)

        @pl.when(jnp.logical_and(match, hits == 0))
        def _():
            out_ref[...] = term()

        @pl.when(jnp.logical_and(match, hits > 0))
        def _():
            @pl.when(hits == 1)
            def _():
                acc[...] = out_ref[...].astype(jnp.float32)

            acc[...] += term().astype(jnp.float32)

        return hits + match.astype(jnp.int32)

    hits = lax.fori_loop(0, batches, step, jnp.int32(0))

    @pl.when(hits == 0)
    def _():
        out_ref[...] = jnp.zeros_like(out_ref)

    @pl.when(hits > 1)
    def _():
        out_ref[...] = acc[...].astype(out_ref.dtype)


def head_grad(block_ids, live_flags, grad_all, hid_all, blocks):
    batches, tokens, block_rows = grad_all.shape
    width = hid_all.shape[2]
    return pl.pallas_call(
        head_body,
        grid_spec=pltpu.PrefetchScalarGridSpec(
            num_scalar_prefetch=2,
            grid=(blocks,),
            in_specs=[
                pl.BlockSpec(grad_all.shape, lambda b, ids, live: (0, 0, 0)),
                pl.BlockSpec(hid_all.shape, lambda b, ids, live: (0, 0, 0)),
            ],
            out_specs=pl.BlockSpec((block_rows, width), lambda b, ids, live: (b, 0)),
            scratch_shapes=[pltpu.VMEM((block_rows, width), jnp.float32)],
        ),
        out_shape=jax.ShapeDtypeStruct((blocks * block_rows, width), jnp.bfloat16),
        compiler_params=pltpu.CompilerParams(vmem_limit_bytes=48 * 2**20),
        cost_estimate=pl.CostEstimate(
            flops=2 * batches * tokens * block_rows * width,
            bytes_accessed=2 * (grad_all.size + hid_all.size + blocks * block_rows * width),
            transcendentals=0,
        ),
    )(block_ids, live_flags, grad_all, hid_all)


MESH = pl.DeviceIdType.MESH


def exchange_body(
    hidden, head, ids, teacher, live, hid_out, grad_out, hid_grad,
    table, hid_all, grad_all, value_all,
    pair_out, pair_in, chip_sum, chip_in, stat_out, stat_in, coef,
    term_out, term_in, term_own, final,
    a1s, a1r, a2s, a2r, cs, cr, zs, zr, ss, sr, gs, gr, fs, e1s, e1r, e2s, e2r, own_sems,
):
    sec = lax.axis_index("section")
    rep = lax.axis_index("dp")
    batches, tokens, width = hid_all.shape
    n_sec = stat_in.shape[0]
    chips = batches // 2
    tok_local = tokens // n_sec
    block_rows = table.shape[1]
    core = lax.rem(rep, 2)
    z = rep // 2
    sib = 2 * z + 1 - core
    f32, bf16 = jnp.float32, jnp.bfloat16

    def chip_at(k):
        return lax.rem(z + k, chips)

    def chip_back(k):
        return lax.rem(z - k + chips, chips)

    def sec_at(j):
        return lax.rem(sec + j, n_sec)

    def rows_of(s):
        return pl.ds(pl.multiple_of(s * tok_local, tok_local), tok_local)

    def cols_of(d):
        return pl.ds(pl.multiple_of(d * width, width), width)

    def loop(lo, hi, body):
        def step(i, carry):
            body(i)
            return carry

        lax.fori_loop(lo, hi, step, 0)

    def remote(src, dst, send, recv, **to):
        return pltpu.make_async_remote_copy(
            src_ref=src, dst_ref=dst, send_sem=send, recv_sem=recv,
            device_id=to, device_id_type=MESH,
        )

    load_head = pltpu.make_async_copy(head, table, own_sems.at[0])
    load_head.start()
    barrier = pltpu.get_barrier_semaphore()

    def hello_dp(k):
        pl.semaphore_signal(barrier, inc=1, device_id={"dp": lax.rem(rep + k, batches)}, device_id_type=MESH)

    def hello_sec(j):
        pl.semaphore_signal(barrier, inc=1, device_id={"section": sec_at(j)}, device_id_type=MESH)

    loop(1, batches, hello_dp)
    loop(1, n_sec, hello_sec)
    pl.semaphore_wait(barrier, batches - 1 + n_sec - 1)

    def piece(to, source):
        return remote(
            hidden.at[0, :, cols_of(to)], hid_all.at[source, rows_of(sec), :],
            a1s.at[to], a1r.at[source], dp=to,
        )

    piece(sib, rep).start()

    def send_piece(k):
        piece(2 * chip_back(k) + core, rep).start()
        piece(2 * chip_back(k) + 1 - core, rep).start()

    loop(1, chips, send_piece)
    hid_all[rep, rows_of(sec), :] = hidden[0, :, cols_of(rep)]

    def spread(m, s_to, s_from, slot):
        block = hid_all.at[m, rows_of(s_from), :]
        return remote(block, block, a2s.at[m, slot], a2r.at[m, s_from], section=s_to)

    def forward(m):
        loop(1, n_sec, lambda j: spread(m, sec_at(j), sec, sec_at(j)).start())

    def arrive(m):
        loop(1, n_sec, lambda j: spread(m, sec_at(j), sec_at(j), sec_at(j)).wait_recv())

    def forward_chip(k):
        for parity in (core, 1 - core):
            m = 2 * chip_at(k) + parity
            piece(sib, m).wait_recv()
            forward(m)

    forward_chip(1)
    forward_chip(2)
    load_head.wait()

    def scores(m):
        return lax.dot_general(
            hid_all[m], table[ids[m]], (((1,), (1,)), ((), ())), preferred_element_type=f32
        )

    def pair(zz):
        return remote(pair_out.at[zz], pair_in.at[zz], cs.at[zz], cr.at[zz], dp=sib)

    def owner(zz, source):
        return remote(
            chip_sum.at[zz], chip_in.at[source], zs.at[zz], zr.at[source], dp=2 * zz + core
        )

    def logits_of(i):
        k = lax.rem(i + 1, chips)

        @pl.when(i < chips - 3)
        def _():
            forward_chip(i + 3)

        @pl.when(i == chips - 3)
        def _():
            forward(rep)
            piece(sib, sib).wait_recv()
            forward(sib)

        zz = chip_at(k)
        away, near = 2 * zz + 1 - core, 2 * zz + core
        arrive(away)
        pair_out[zz] = scores(away)
        pair(zz).start()
        arrive(near)
        value = scores(near)
        pair(zz).wait_recv()
        chip_sum[zz] = value + pair_in[zz]

        @pl.when(k > 0)
        def _():
            owner(zz, z).start()

    loop(0, chips, logits_of)
    save_hid = pltpu.make_async_copy(hid_all, hid_out, own_sems.at[1])
    save_hid.start()

    def collect(k):
        owner(chip_at(k), chip_at(k)).wait_recv()
        chip_sum[z] = chip_sum[z] + chip_in[chip_at(k)]

    loop(1, chips, collect)

    logits = chip_sum[z]
    teach = teacher[0].astype(f32)
    s_max = jnp.max(logits, axis=1, keepdims=True)
    t_max = jnp.max(teach, axis=1, keepdims=True)
    s_exp = jnp.exp(logits - s_max)
    t_exp = jnp.exp(teach - t_max)
    s_sum = jnp.sum(s_exp, axis=1, keepdims=True)
    t_sum = jnp.sum(t_exp, axis=1, keepdims=True)
    lane = lax.broadcasted_iota(jnp.int32, (tokens, 128), 1)
    stats = jnp.where(lane == 0, s_max, 0.0)
    stats = jnp.where(lane == 1, s_sum, stats)
    stats = jnp.where(lane == 2, t_max, stats)
    stats = jnp.where(lane == 3, t_sum, stats)
    rows = stats.T[:8]
    row_at = lax.broadcasted_iota(jnp.int32, rows.shape, 0)
    rows = jnp.where(row_at == 4, live[...], rows)
    stat_out[...] = rows
    stat_in[sec] = rows

    def stat(s_to, s_from):
        return remote(stat_out, stat_in.at[s_from], ss.at[s_to], sr.at[s_from], section=s_to)

    loop(1, n_sec, lambda j: stat(sec_at(j), sec).start())
    loop(1, n_sec, lambda j: stat(sec_at(j), sec_at(j)).wait_recv())
    alive = [stat_in[i, 4:5, :] for i in range(n_sec)]
    count = functools.reduce(jnp.add, alive)

    def merged(at):
        tops = [jnp.where(a > 0, stat_in[i, at : at + 1, :], neg_fill) for i, a in enumerate(alive)]
        top = functools.reduce(jnp.maximum, tops)
        total = functools.reduce(
            jnp.add,
            [
                jnp.where(a > 0, stat_in[i, at + 1 : at + 2, :] * jnp.exp(tops[i] - top), 0.0)
                for i, a in enumerate(alive)
            ],
        )
        own = stat_in[sec]
        own_alive = own[4:5, :] > 0
        own_top = jnp.where(own_alive, own[at : at + 1, :], neg_fill)
        return jnp.where(own_alive, block_rows * count * (jnp.exp(own_top - top) / total), 0.0)

    coef[...] = jnp.zeros_like(coef)
    coef[0:1, :] = merged(0)
    coef[1:2, :] = merged(2)
    turned = coef[...].T
    grad_all[rep] = (s_exp * turned[:, 0:1] - t_exp * turned[:, 1:2]).astype(bf16)

    def share(zz, m):
        return remote(grad_all.at[m], grad_all.at[m], gs.at[zz], gr.at[m], dp=2 * zz + core)

    def relay(m):
        return remote(grad_all.at[m], grad_all.at[m], fs.at[m // 2], gr.at[m], dp=sib)

    relay(rep).start()
    loop(1, chips, lambda k: share(chip_back(k), rep).start())

    def term(m, s_to, s_from):
        return remote(
            term_out.at[m, rows_of(s_to), :], term_in.at[m, s_from],
            e1s.at[m, s_to], e1r.at[m, s_from], section=s_to,
        )

    def terms_of(m):
        value = lax.dot_general(
            grad_all[m], table[ids[m]], (((1,), (0,)), ((), ())), preferred_element_type=f32
        )
        value_all[...] = value
        term_out[m] = value.astype(bf16)
        loop(1, n_sec, lambda j: term(m, sec_at(j), sec).start())
        term_own[m] = value_all[rows_of(sec), :]

    def terms_chip(k):
        near, away = 2 * chip_at(k) + core, 2 * chip_at(k) + 1 - core

        @pl.when(k > 0)
        def _():
            share(chip_at(k), near).wait_recv()
            relay(near).start()

        terms_of(near)
        relay(away).wait_recv()
        terms_of(away)

    def home(m, source):
        return remote(
            final.at[m], hid_grad.at[:, cols_of(source)], e2s.at[m], e2r.at[source], dp=m
        )

    def summed(m):
        loop(1, n_sec, lambda j: term(m, sec_at(j), sec_at(j)).wait_recv())

        def add(j):
            term_own[m] = term_own[m] + term_in[m, sec_at(j)].astype(f32)

        loop(1, n_sec, add)
        return term_own[m].astype(bf16)

    def finish(k):
        near, away = 2 * chip_at(k) + core, 2 * chip_at(k) + 1 - core
        final[near] = summed(near)

        @pl.when(k > 0)
        def _():
            home(near, rep).start()

        final[away] = summed(away)
        home(away, rep).start()

    def stage(i):
        @pl.when(i < chips)
        def _():
            terms_chip(i)

        @pl.when(i > 1)
        def _():
            finish(i - 2)

    loop(0, chips, stage)
    save_grad = pltpu.make_async_copy(grad_all, grad_out, own_sems.at[2])
    save_grad.start()
    loop(chips, chips + 2, stage)
    hid_grad[:, cols_of(rep)] = final[rep]

    def ends_dp(k):
        other = lax.rem(rep + k, batches)
        home(other, other).wait_recv()
        home(other, rep).wait_send()
        piece(other, rep).wait_send()

    loop(1, batches, ends_dp)

    def ends_all(m):
        def each(j):
            spread(m, sec_at(j), sec, sec_at(j)).wait_send()
            term(m, sec_at(j), sec).wait_send()

        loop(1, n_sec, each)

    loop(0, batches, ends_all)
    loop(1, n_sec, lambda j: stat(sec_at(j), sec).wait_send())

    def ends_chip(k):
        pair(chip_at(k)).wait_send()
        relay(2 * chip_at(k) + core).wait_send()

        @pl.when(k > 0)
        def _():
            owner(chip_at(k), z).wait_send()
            share(chip_at(k), rep).wait_send()

    loop(0, chips, ends_chip)
    save_hid.wait()
    save_grad.wait()


def exchange(hidden, table, ids, teacher, live, n_sec):
    tok_local, model_width = hidden.shape[1], hidden.shape[2]
    blocks, block_rows, width = table.shape
    batches = ids.shape[0]
    tokens = teacher.shape[1]
    chips = batches // 2
    dma = pltpu.SemaphoreType.DMA
    f32, bf16 = jnp.float32, jnp.bfloat16
    vmem = pl.BlockSpec(memory_space=pltpu.VMEM)
    smem = pl.BlockSpec(memory_space=pltpu.SMEM)
    hbm = pl.BlockSpec(memory_space=pl.ANY)
    return pl.pallas_call(
        exchange_body,
        out_shape=(
            jax.ShapeDtypeStruct((batches, tokens, width), bf16),
            jax.ShapeDtypeStruct((batches, tokens, block_rows), bf16),
            jax.ShapeDtypeStruct((tok_local, model_width), bf16),
        ),
        in_specs=[vmem, hbm, smem, vmem, vmem],
        out_specs=(hbm, hbm, vmem),
        scratch_shapes=[
            pltpu.VMEM((blocks, block_rows, width), bf16),
            pltpu.VMEM((batches, tokens, width), bf16),
            pltpu.VMEM((batches, tokens, block_rows), bf16),
            pltpu.VMEM((tokens, width), f32),
            pltpu.VMEM((chips, tokens, block_rows), f32),
            pltpu.VMEM((chips, tokens, block_rows), f32),
            pltpu.VMEM((chips, tokens, block_rows), f32),
            pltpu.VMEM((chips, tokens, block_rows), f32),
            pltpu.VMEM((8, tokens), f32),
            pltpu.VMEM((n_sec, 8, tokens), f32),
            pltpu.VMEM((128, tokens), f32),
            pltpu.VMEM((batches, tokens, width), bf16),
            pltpu.VMEM((batches, n_sec, tok_local, width), bf16),
            pltpu.VMEM((batches, tok_local, width), f32),
            pltpu.VMEM((batches, tok_local, width), bf16),
            dma((batches,)), dma((batches,)),
            dma((batches, n_sec)), dma((batches, n_sec)),
            dma((chips,)), dma((chips,)),
            dma((chips,)), dma((chips,)),
            dma((n_sec,)), dma((n_sec,)),
            dma((chips,)), dma((batches,)), dma((chips,)),
            dma((batches, n_sec)), dma((batches, n_sec)),
            dma((batches,)), dma((batches,)), dma((3,)),
        ],
        compiler_params=pltpu.CompilerParams(
            collective_id=0, has_side_effects=True, vmem_limit_bytes=60 * 2**20
        ),
        cost_estimate=pl.CostEstimate(
            flops=4 * batches * tokens * block_rows * width,
            bytes_accessed=2 * batches * block_rows * width,
            transcendentals=0,
        ),
    )(hidden, table, ids, teacher, live)


def local(hidden, head, block_id, block_live, teacher, n_sec):
    my_replica = lax.axis_index("dp")
    tokens, block_rows = teacher.shape[1], teacher.shape[2]
    blocks = head.shape[0] // block_rows
    block_ids = block_id[:, 0]
    live_flags = block_live[:, 0]
    table = head.reshape(blocks, block_rows, head.shape[1])
    own_live = lax.dynamic_index_in_dim(live_flags, my_replica, 0, keepdims=False) > 0
    live = jnp.broadcast_to(jnp.where(own_live, 1.0, 0.0).astype(jnp.float32), (8, tokens))
    hid_all, grad_all, hid_grad = exchange(hidden, table, block_ids, teacher, live, n_sec)
    grad_head = head_grad(block_ids, live_flags, grad_all, hid_all, blocks)
    return (hid_grad[None], grad_head)


def solution(mesh):
    placed = (
        P("dp", "section", None),
        P("section", "dp"),
        P(None, "section"),
        P(None, "section"),
        P("dp", None, "section"),
    )
    return jax.shard_map(
        functools.partial(local, n_sec=mesh.shape["section"]),
        mesh=mesh,
        in_specs=placed,
        out_specs=(P("dp", "section", None), P("section", "dp")),
        check_vma=False,
    )
```
